32 devices in a mesh: row: 4 (over y, x), col: 8 (over z, core).
Axes of the slice: x: 2, y: 2, z: 4, core: 2. Of those that a mesh axis runs over, the one named last changes fastest.
Arguments:
- tokens_b: bfloat16 [512, 12288], P('col', 'row'), may hold values from -6 to 6
- tokens_a: bfloat16 [512, 12288], P('col', 'row'), may hold values from -6 to 6
- upstream_a: bfloat16 [512, 12288], P('col', 'row'), may hold values from -1.5 to 1.5
- up_weight: bfloat16 [12288, 24576], P('row', 'col'), may hold values from -0.0546875 to 0.0546875
- down_weight: bfloat16 [24576, 12288], P('col', 'row'), may hold values from -0.0390625 to 0.0390625
Outputs:
- output_b: bfloat16 [512, 12288], P('col', 'row')
- input_grad: bfloat16 [512, 12288], P('col', 'row')
- up_grad: bfloat16 [12288, 24576], P('row', 'col')
- down_grad: bfloat16 [24576, 12288], P('col', 'row')
The draws below stay inside these ranges and needn't reach their ends.
All inputs are finite; a program needn't handle non-finite values.
Results may differ from the reference program's by a relative error of at most 0.02.
Values may be sent and summed in bfloat16 or wider, within the bound.
A program may use at most 192 MiB of HBM per device.

```python
import jax
import jax.numpy as jnp
from jax import lax

D = 12288
FF = 24576
TOKENS = 512
N_ROW = 4
N_COL = 8


def block_scale(rng, shape, pieces, least, largest):
    def one(axis_at, blocks):
        draws = jax.random.uniform(jax.random.fold_in(jax.random.fold_in(rng, 6), axis_at), (blocks,), jnp.float32, least / len(pieces), largest / len(pieces))
        return jnp.repeat(jnp.exp(draws), shape[axis_at] // blocks).reshape((-1,) + (1,) * (len(shape) - axis_at - 1))

    level = one(*pieces[0])
    for cut in pieces[1:]:
        level = level * one(*cut)
    return level


def bell_draw(own_key, shape, spread, limit, shards=(), held_as=jnp.bfloat16):
    array = jax.random.normal(own_key, shape, jnp.float32) * spread
    if len(shards) > 0:
        array = block_scale(own_key, shape, shards, -0.22, 0.18) * array
    return jnp.clip(array, min=-limit, max=limit).astype(held_as)


def setup_inputs(seed: int = 0) -> dict:
    arg_keys = jax.random.split(jax.random.key(seed), 6)
    return {
        "tokens_b": bell_draw(arg_keys[0], (TOKENS, D), 1.0, 6.0, ((0, 8), (1, 4))),
        "tokens_a": bell_draw(arg_keys[1], (TOKENS, D), 1.0, 6.0, ((0, 8), (1, 4))),
        "upstream_a": bell_draw(arg_keys[2], (TOKENS, D), 0.25, 1.5, ((0, 8), (1, 4))),
        "up_weight": bell_draw(arg_keys[3], (D, FF), D ** -0.5, 0.0546875, ((0, 4), (1, 8))),
        "down_weight": bell_draw(arg_keys[4], (FF, D), FF ** -0.5, 0.0390625, ((0, 8), (1, 4))),
    }


def smooth_gate(value):
    return jax.nn.gelu(value, approximate=True)

def grouped(left, right, groups):
    count = left.shape[0]
    inner = left.shape[1]
    width = right.shape[1]
    lefts = left.reshape(count, groups, inner // groups).transpose(1, 0, 2)
    rights = right.reshape(groups, inner // groups, width)

    def step(total, pair):
        part = jnp.dot(pair[0], pair[1], preferred_element_type=jnp.float32)
        rounded = lax.optimization_barrier(part.astype(jnp.bfloat16))
        return (total + rounded.astype(jnp.float32), None)
    total, _ = lax.scan(step, jnp.zeros((count, width), jnp.float32), (lefts, rights))
    return total

def reference(tokens_b, tokens_a, upstream_a, up_weight, down_weight):
    hidden_b = grouped(tokens_b, up_weight, N_ROW)
    gated_b = smooth_gate(hidden_b).astype(jnp.bfloat16)
    output_b = grouped(gated_b, down_weight, N_COL).astype(jnp.bfloat16)
    hidden_a = grouped(tokens_a, up_weight, N_ROW)
    grad_gate = grouped(upstream_a, down_weight.T, N_ROW)
    gated_full, pullback = jax.vjp(smooth_gate, hidden_a)
    grad_pre = pullback(grad_gate)[0].astype(jnp.bfloat16)
    gated_a = gated_full.astype(jnp.bfloat16)
    input_grad = grouped(grad_pre, up_weight.T, N_COL).astype(jnp.bfloat16)
    up_grad = jnp.dot(tokens_a.T, grad_pre, preferred_element_type=jnp.float32).astype(jnp.bfloat16)
    down_grad = jnp.dot(gated_a.T, upstream_a, preferred_element_type=jnp.float32).astype(jnp.bfloat16)
    return (output_b, input_grad, up_grad, down_grad)
```

```python
import functools

import jax
import jax.numpy as jnp
from jax import lax
from jax.experimental import pallas as pl
from jax.experimental.pallas import tpu as pltpu
from jax.sharding import PartitionSpec as P

BF = jnp.bfloat16
F32 = jnp.float32
MESH = pl.DeviceIdType.MESH
SCALE = 0.7978845608028654
CUBIC = 0.044715


def gelu(v):
    return 0.5 * v * (1.0 + jnp.tanh(SCALE * (v + CUBIC * (v * v * v))))


def gelu_both(v):
    t = jnp.tanh(SCALE * (v + CUBIC * (v * v * v)))
    half = 0.5 * (1.0 + t)
    slope = half + 0.5 * v * (1.0 - t * t) * (SCALE * (1.0 + (3.0 * CUBIC) * (v * v)))
    return v * half, slope


def kernel(
    nr, nc, chunk, groups,
    tok_b, tok_a, ups, w_up, w_down,
    out_b, in_grad, all_a, all_u, all_ga, all_gp,
    t_buf, p_buf, r_buf, g_buf, o_buf, sib_buf, z_buf, w_col, w_row,
    ag_send, ag_recv, fw_send, fw_recv, rs_send, rs_recv, rg_send, rg_recv,
    sb_send, sb_recv, zs_send, zs_recv, loc_sem, w_sem, out_sem,
):
    nz = nc // 2
    row = lax.axis_index("row")
    col = lax.axis_index("col")
    z, core = col // 2, col % 2
    tb = tok_b.shape[0]
    width = tok_b.shape[1]
    ff = w_up.shape[1]
    tokens = tb * nc
    rb = tokens // nr
    sibling = (row, z * 2 + 1 - core)

    def rpeer(k):
        return lax.rem(row + k, nr)

    def zpeer(k):
        return lax.rem(z + k, nz)

    def rows_of(index, size):
        return pl.ds(pl.multiple_of(index * size, size), size)

    def cols_of(index, size):
        return pl.ds(pl.multiple_of(index * size, 128), size)

    barrier = pltpu.get_barrier_semaphore()
    for k in range(1, nr):
        pl.semaphore_signal(barrier, inc=1, device_id=(rpeer(k), col), device_id_type=MESH)
    for k in range(1, nz):
        pl.semaphore_signal(barrier, inc=1, device_id=(row, zpeer(k) * 2 + core), device_id_type=MESH)
    pl.semaphore_signal(barrier, inc=1, device_id=sibling, device_id_type=MESH)
    pl.semaphore_wait(barrier, nr - 1 + nz)

    def remote(src, dst, send, recv, device):
        return pltpu.make_async_remote_copy(
            src_ref=src, dst_ref=dst, send_sem=send, recv_sem=recv, device_id=device, device_id_type=MESH
        )

    mine = rows_of(col, tb)
    sources = (tok_b, tok_a, ups)
    gather = []
    for s in range(3):
        pltpu.make_async_copy(sources[s], t_buf.at[s, mine, :], loc_sem.at[s]).start()
        one = []
        for k in range(1, nz):
            c = remote(sources[s], t_buf.at[s, mine, :], ag_send.at[s, k], ag_recv.at[s, k],
                       (row, zpeer(k) * 2 + core))
            c.start()
            one.append(c)
        c = remote(sources[s], t_buf.at[s, mine, :], fw_send.at[s, 0], fw_recv.at[s, 0], sibling)
        c.start()
        gather.append((one, c))

    forwards = []

    def arrive(s):
        mine_now = []
        for k in range(1, nz):
            gather[s][0][k - 1].wait_recv()
            block = rows_of(lax.rem(z + nz - k, nz) * 2 + core, tb)
            c = remote(t_buf.at[s, block, :], t_buf.at[s, block, :], fw_send.at[s, k], fw_recv.at[s, k], sibling)
            c.start()
            mine_now.append(c)
        pltpu.make_async_copy(sources[s], t_buf.at[s, mine, :], loc_sem.at[s]).wait()
        gather[s][1].wait_recv()
        for c in mine_now:
            c.wait_recv()
        forwards.extend(mine_now)

    def up_cols(j):
        return w_up.at[:, cols_of(j, chunk)], w_col

    def up_rows(j):
        return w_up.at[rows_of(j, chunk), :], w_row

    def down_cols(j):
        return w_down.at[:, cols_of(j, chunk)], w_col

    def down_rows(j):
        return w_down.at[rows_of(j, chunk), :], w_row

    def products(steps, weight, flip, left, target, after):
        def load(j):
            src, buf = weight(j)
            slot = lax.rem(j, 2)
            return pltpu.make_async_copy(src, buf.at[slot], w_sem.at[slot])

        load(0).start()

        def step(j, _):
            @pl.when(j + 1 < steps)
            def _():
                load(j + 1).start()

            load(j).wait()
            block = (w_row if flip else w_col)[lax.rem(j, 2)]
            dims = (((1,), (1 if flip else 0,)), ((), ()))
            got = lax.dot_general(left[...], block, dims, preferred_element_type=F32)
            target[:, cols_of(j, chunk)] = got.astype(BF)
            after(j)
            return 0

        lax.fori_loop(0, steps, step, 0)

    steps = ff // chunk
    per = steps // groups
    gw = per * chunk

    def send_sum(s):
        def after(j):
            g = j // per
            for k in range(1, nr):
                where = rows_of(rpeer(k), rb)
                remote(p_buf.at[s, where, cols_of(j, chunk)], r_buf.at[s, k - 1, :, cols_of(j, chunk)],
                       rs_send.at[s, k], rs_recv.at[s, g, k], (rpeer(k), col)).start()
        return after

    own_rows = rows_of(row, rb)

    def total(s, g):
        cols = cols_of(g, gw)
        for k in range(1, nr):
            view = r_buf.at[s, k - 1, :, cols]
            remote(view, view, rs_send.at[s, k], rs_recv.at[s, g, k], (rpeer(k), col)).wait_recv()
        value = p_buf[s, own_rows, cols].astype(F32)
        for k in range(1, nr):
            value += r_buf[s, k - 1, :, cols].astype(F32)
        return value

    def share(s, g):
        cols = cols_of(g, gw)
        for k in range(1, nr):
            view = g_buf.at[s, own_rows, cols]
            remote(view, view, rg_send.at[s, k], rg_recv.at[s, k], (rpeer(k), col)).start()

    def activate_b(g, _):
        g_buf[0, own_rows, cols_of(g, gw)] = gelu(total(0, g)).astype(BF)
        share(0, g)
        return 0

    def activate_a(g, _):
        value, slope = gelu_both(total(1, g))
        g_buf[1, own_rows, cols_of(g, gw)] = value.astype(BF)
        g_buf[2, own_rows, cols_of(g, gw)] = (total(2, g) * slope).astype(BF)
        share(2, g)
        return 0

    def share_a(g, _):
        share(1, g)
        return 0

    def shared(s):
        for k in range(1, nr):
            view = g_buf.at[s, rows_of(lax.rem(row + nr - k, nr), rb), :]
            remote(view, view, rg_send.at[s, k], rg_recv.at[s, k], (rpeer(k), col)).wait_recv()

    osteps = width // chunk
    oper = osteps // groups
    ow = oper * chunk

    def send_sibling(o):
        def after(j):
            g = j // oper
            for k in range(nz):
                where = rows_of(k * 2 + 1 - core, tb)
                remote(o_buf.at[o, where, cols_of(j, chunk)], sib_buf.at[o, k, :, cols_of(j, chunk)],
                       sb_send.at[o], sb_recv.at[o, g], sibling).start()
        return after

    def combine(o):
        def step(g, _):
            cols = cols_of(g, ow)
            view = sib_buf.at[o, :, :, cols]
            remote(view, view, sb_send.at[o], sb_recv.at[o, g], sibling).wait_recv()
            for k in range(nz):
                where = rows_of(zpeer(k) * 2 + core, tb)
                both = o_buf[o, where, cols].astype(F32) + sib_buf[o, zpeer(k), :, cols].astype(F32)
                o_buf[o, where, cols] = both.astype(BF)
                if k > 0:
                    remote(o_buf.at[o, where, cols], z_buf.at[o, k - 1, :, cols], zs_send.at[o, k],
                           zs_recv.at[o, g, k], (row, zpeer(k) * 2 + core)).start()
            return 0

        lax.fori_loop(0, groups, step, 0)

    def finish(o, target):
        def step(g, _):
            cols = cols_of(g, ow)
            value = o_buf[o, mine, cols].astype(F32)
            for k in range(1, nz):
                view = z_buf.at[o, k - 1, :, cols]
                remote(view, view, zs_send.at[o, k], zs_recv.at[o, g, k], (row, zpeer(k) * 2 + core)).wait_recv()
                value += z_buf[o, k - 1, :, cols].astype(F32)
            target[:, cols] = value.astype(BF)
            return 0

        lax.fori_loop(0, groups, step, 0)

    arrive(0)
    products(steps, up_cols, False, t_buf.at[0], p_buf.at[0], send_sum(0))
    arrive(1)
    products(steps, up_cols, False, t_buf.at[1], p_buf.at[1], send_sum(1))
    lax.fori_loop(0, groups, activate_b, 0)
    arrive(2)
    products(steps, down_rows, True, t_buf.at[2], p_buf.at[2], send_sum(2))
    kept = [
        pltpu.make_async_copy(t_buf.at[1], all_a, out_sem.at[0]),
        pltpu.make_async_copy(t_buf.at[2], all_u, out_sem.at[1]),
    ]
    kept[0].start()
    kept[1].start()
    shared(0)
    products(osteps, down_cols, False, g_buf.at[0], o_buf.at[0], send_sibling(0))
    combine(0)
    lax.fori_loop(0, groups, activate_a, 0)
    lax.fori_loop(0, groups, share_a, 0)
    shared(2)
    products(osteps, up_rows, True, g_buf.at[2], o_buf.at[1], send_sibling(1))
    combine(1)
    kept.append(pltpu.make_async_copy(g_buf.at[2], all_gp, out_sem.at[2]))
    kept[2].start()
    finish(0, out_b)
    shared(1)
    kept.append(pltpu.make_async_copy(g_buf.at[1], all_ga, out_sem.at[3]))
    kept[3].start()
    finish(1, in_grad)

    for c in kept:
        c.wait()
    for s in range(3):
        for c in gather[s][0]:
            c.wait_send()
        gather[s][1].wait_send()
    for c in forwards:
        c.wait_send()
    for s in range(3):
        for k in range(1, nr):
            view = p_buf.at[s, rows_of(rpeer(k), rb), :]
            remote(view, view, rs_send.at[s, k], rg_recv.at[s, k], (rpeer(k), col)).wait_send()
            view = g_buf.at[s, own_rows, :]
            remote(view, view, rg_send.at[s, k], rg_recv.at[s, k], (rpeer(k), col)).wait_send()
    for o in range(2):
        view = sib_buf.at[o]
        remote(view, view, sb_send.at[o], sb_recv.at[o, 0], sibling).wait_send()
        for k in range(1, nz):
            view = o_buf.at[o, rows_of(zpeer(k) * 2 + core, tb), :]
            remote(view, view, zs_send.at[o, k], zs_recv.at[o, 0, k], (row, zpeer(k) * 2 + core)).wait_send()


def exchange(nr, nc, tokens_b, tokens_a, upstream_a, up_weight, down_weight):
    tb, width = tokens_b.shape
    ff = up_weight.shape[1]
    tokens = tb * nc
    rb = tokens // nr
    nz = nc // 2
    chunk = 256
    groups = next(g for g in (4, 3, 2, 1) if (ff // chunk) % g == 0 and (width // chunk) % g == 0)
    dma = pltpu.SemaphoreType.DMA
    anywhere = pl.BlockSpec(memory_space=pl.ANY)
    near = pl.BlockSpec(memory_space=pltpu.VMEM)
    whole = jax.ShapeDtypeStruct((tokens, width), BF)
    hidden = jax.ShapeDtypeStruct((tokens, ff), BF)
    block = jax.ShapeDtypeStruct((tb, width), BF)
    return pl.pallas_call(
        functools.partial(kernel, nr, nc, chunk, groups),
        out_shape=(block, block, whole, whole, hidden, hidden),
        in_specs=[anywhere] * 5,
        out_specs=(near, near, anywhere, anywhere, anywhere, anywhere),
        scratch_shapes=[
            pltpu.VMEM((3, tokens, width), BF),
            pltpu.VMEM((3, tokens, ff), BF),
            pltpu.VMEM((3, nr - 1, rb, ff), BF),
            pltpu.VMEM((3, tokens, ff), BF),
            pltpu.VMEM((2, tokens, width), BF),
            pltpu.VMEM((2, nz, tb, width), BF),
            pltpu.VMEM((2, nz - 1, tb, width), BF),
            pltpu.VMEM((2, max(width, ff), chunk), BF),
            pltpu.VMEM((2, chunk, max(width, ff)), BF),
            dma((3, nz)), dma((3, nz)), dma((3, nz)), dma((3, nz)),
            dma((3, nr)), dma((3, groups, nr)), dma((3, nr)), dma((3, nr)),
            dma((2,)), dma((2, groups)), dma((2, nz)), dma((2, groups, nz)),
            dma((3,)), dma((2,)), dma((4,)),
        ],
        compiler_params=pltpu.CompilerParams(
            collective_id=0, has_side_effects=True, vmem_limit_bytes=62 * 1024 * 1024
        ),
        cost_estimate=pl.CostEstimate(
            flops=10 * tokens * width * ff, bytes_accessed=8 * width * ff, transcendentals=0
        ),
    )(tokens_b, tokens_a, upstream_a, up_weight, down_weight)


def on_device(nr, nc, tokens_b, tokens_a, upstream_a, up_weight, down_weight):
    output_b, input_grad, inputs_a, upstream, gated_a, grad_pre = exchange(
        nr, nc, tokens_b, tokens_a, upstream_a, up_weight, down_weight
    )
    up_grad = lax.dot_general(inputs_a, grad_pre, (((0,), (0,)), ((), ())), preferred_element_type=F32)
    down_grad = lax.dot_general(gated_a, upstream, (((0,), (0,)), ((), ())), preferred_element_type=F32)
    return output_b, input_grad, up_grad.astype(BF), down_grad.astype(BF)


def solution(mesh):
    placed = (P("col", "row"), P("col", "row"), P("col", "row"), P("row", "col"), P("col", "row"))
    return jax.shard_map(
        functools.partial(on_device, mesh.shape["row"], mesh.shape["col"]),
        mesh=mesh,
        in_specs=placed,
        out_specs=(P("col", "row"), P("col", "row"), P("row", "col"), P("col", "row")),
        check_vma=False,
    )
```

```python
import functools

import jax
import jax.numpy as jnp
from jax import lax
from jax.experimental import pallas as pl
from jax.experimental.pallas import tpu as pltpu
from jax.sharding import PartitionSpec as P

BF = jnp.bfloat16
F32 = jnp.float32
MESH = pl.DeviceIdType.MESH
SCALE = 0.7978845608028654
CUBIC = 0.044715


def gelu(v):
    return 0.5 * v * (1.0 + jnp.tanh(SCALE * (v + CUBIC * (v * v * v))))


def gelu_both(v):
    t = jnp.tanh(SCALE * (v + CUBIC * (v * v * v)))
    half = 0.5 * (1.0 + t)
    slope = half + 0.5 * v * (1.0 - t * t) * (SCALE * (1.0 + (3.0 * CUBIC) * (v * v)))
    return v * half, slope


def kernel(
    nr, nc, chunk, groups,
    tok_b, tok_a, ups, w_up, w_down,
    out_b, in_grad, all_a, all_u, all_ga, all_gp,
    t_buf, p_buf, r_buf, g_buf, o_buf, sib_buf, z_buf, w_col, w_row,
    ag_send, ag_recv, fw_send, fw_recv, rs_send, rs_recv, rg_send, rg_recv,
    sb_send, sb_recv, zs_send, zs_recv, loc_sem, w_sem, out_sem,
):
    nz = nc // 2
    row = lax.axis_index("row")
    col = lax.axis_index("col")
    z, core = col // 2, col % 2
    tb = tok_b.shape[0]
    width = tok_b.shape[1]
    ff = w_up.shape[1]
    tokens = tb * nc
    rb = tokens // nr
    sibling = (row, z * 2 + 1 - core)

    def rpeer(k):
        return lax.rem(row + k, nr)

    def zpeer(k):
        return lax.rem(z + k, nz)

    def rows_of(index, size):
        return pl.ds(pl.multiple_of(index * size, size), size)

    def cols_of(index, size):
        return pl.ds(pl.multiple_of(index * size, 128), size)

    barrier = pltpu.get_barrier_semaphore()
    for k in range(1, nr):
        pl.semaphore_signal(barrier, inc=1, device_id=(rpeer(k), col), device_id_type=MESH)
    for k in range(1, nz):
        pl.semaphore_signal(barrier, inc=1, device_id=(row, zpeer(k) * 2 + core), device_id_type=MESH)
    pl.semaphore_signal(barrier, inc=1, device_id=sibling, device_id_type=MESH)
    pl.semaphore_wait(barrier, nr - 1 + nz)

    def remote(src, dst, send, recv, device):
        return pltpu.make_async_remote_copy(
            src_ref=src, dst_ref=dst, send_sem=send, recv_sem=recv, device_id=device, device_id_type=MESH
        )

    mine = rows_of(col, tb)
    sources = (tok_b, tok_a, ups)
    gather = []
    for s in range(3):
        pltpu.make_async_copy(sources[s], t_buf.at[s, mine, :], loc_sem.at[s]).start()
        one = []
        for k in range(1, nz):
            c = remote(sources[s], t_buf.at[s, mine, :], ag_send.at[s, k], ag_recv.at[s, k],
                       (row, zpeer(k) * 2 + core))
            c.start()
            one.append(c)
        c = remote(sources[s], t_buf.at[s, mine, :], fw_send.at[s, 0], fw_recv.at[s, 0], sibling)
        c.start()
        gather.append((one, c))

    forwards = []

    def arrive(s):
        mine_now = []
        for k in range(1, nz):
            gather[s][0][k - 1].wait_recv()
            block = rows_of(lax.rem(z + nz - k, nz) * 2 + core, tb)
            c = remote(t_buf.at[s, block, :], t_buf.at[s, block, :], fw_send.at[s, k], fw_recv.at[s, k], sibling)
            c.start()
            mine_now.append(c)
        pltpu.make_async_copy(sources[s], t_buf.at[s, mine, :], loc_sem.at[s]).wait()
        gather[s][1].wait_recv()
        for c in mine_now:
            c.wait_recv()
        forwards.extend(mine_now)

    def up_cols(j):
        return w_up.at[:, cols_of(j, chunk)], w_col

    def up_rows(j):
        return w_up.at[rows_of(j, chunk), :], w_row

    def down_cols(j):
        return w_down.at[:, cols_of(j, chunk)], w_col

    def down_rows(j):
        return w_down.at[rows_of(j, chunk), :], w_row

    def products(steps, weight, flip, left, target, after):
        def load(j):
            src, buf = weight(j)
            slot = lax.rem(j, 2)
            return pltpu.make_async_copy(src, buf.at[slot], w_sem.at[slot])

        load(0).start()

        def step(j, _):
            @pl.when(j + 1 < steps)
            def _():
                load(j + 1).start()

            load(j).wait()
            block = (w_row if flip else w_col)[lax.rem(j, 2)]
            dims = (((1,), (1 if flip else 0,)), ((), ()))
            got = lax.dot_general(left[...], block, dims, preferred_element_type=F32)
            target[:, cols_of(j, chunk)] = got.astype(BF)
            after(j)
            return 0

        lax.fori_loop(0, steps, step, 0)

    steps = ff // chunk
    per = steps // groups
    gw = per * chunk

    def send_sum(s):
        def after(j):
            g = j // per
            for k in range(1, nr):
                where = rows_of(rpeer(k), rb)
                remote(p_buf.at[s, where, cols_of(j, chunk)], r_buf.at[s, k - 1, :, cols_of(j, chunk)],
                       rs_send.at[s, k], rs_recv.at[s, g, k], (rpeer(k), col)).start()
        return after

    own_rows = rows_of(row, rb)

    def total(s, g):
        cols = cols_of(g, gw)
        for k in range(1, nr):
            view = r_buf.at[s, k - 1, :, cols]
            remote(view, view, rs_send.at[s, k], rs_recv.at[s, g, k], (rpeer(k), col)).wait_recv()
        value = p_buf[s, own_rows, cols].astype(F32)
        for k in range(1, nr):
            value += r_buf[s, k - 1, :, cols].astype(F32)
        return value

    def share(s, g):
        cols = cols_of(g, gw)
        for k in range(1, nr):
            view = g_buf.at[s, own_rows, cols]
            remote(view, view, rg_send.at[s, k], rg_recv.at[s, k], (rpeer(k), col)).start()

    def activate_b(g, _):
        g_buf[0, own_rows, cols_of(g, gw)] = gelu(total(0, g)).astype(BF)
        share(0, g)
        return 0

    def activate_a(g, _):
        value, slope = gelu_both(total(1, g))
        g_buf[1, own_rows, cols_of(g, gw)] = value.astype(BF)
        g_buf[2, own_rows, cols_of(g, gw)] = (total(2, g) * slope).astype(BF)
        share(2, g)
        return 0

    def share_a(g, _):
        share(1, g)
        return 0

    def shared(s):
        for k in range(1, nr):
            view = g_buf.at[s, rows_of(lax.rem(row + nr - k, nr), rb), :]
            remote(view, view, rg_send.at[s, k], rg_recv.at[s, k], (rpeer(k), col)).wait_recv()

    osteps = width // chunk
    oper = osteps // groups
    ow = oper * chunk

    def send_sibling(o):
        def after(j):
            g = j // oper
            for k in range(nz):
                where = rows_of(k * 2 + 1 - core, tb)
                remote(o_buf.at[o, where, cols_of(j, chunk)], sib_buf.at[o, k, :, cols_of(j, chunk)],
                       sb_send.at[o], sb_recv.at[o, g], sibling).start()

            @pl.when(jnp.logical_and(lax.rem(j, oper) == oper - 1, g > 0))
            def _():
                combine(o, g - 1)
        return after

    def combine(o, g):
        cols = cols_of(g, ow)
        view = sib_buf.at[o, :, :, cols]
        remote(view, view, sb_send.at[o], sb_recv.at[o, g], sibling).wait_recv()
        for k in range(nz):
            where = rows_of(zpeer(k) * 2 + core, tb)
            both = o_buf[o, where, cols].astype(F32) + sib_buf[o, zpeer(k), :, cols].astype(F32)
            o_buf[o, where, cols] = both.astype(BF)
            if k > 0:
                remote(o_buf.at[o, where, cols], z_buf.at[o, k - 1, :, cols], zs_send.at[o, k],
                       zs_recv.at[o, g, k], (row, zpeer(k) * 2 + core)).start()

    def finish(o, target):
        def step(g, _):
            cols = cols_of(g, ow)
            value = o_buf[o, mine, cols].astype(F32)
            for k in range(1, nz):
                view = z_buf.at[o, k - 1, :, cols]
                remote(view, view, zs_send.at[o, k], zs_recv.at[o, g, k], (row, zpeer(k) * 2 + core)).wait_recv()
                value += z_buf[o, k - 1, :, cols].astype(F32)
            target[:, cols] = value.astype(BF)
            return 0

        lax.fori_loop(0, groups, step, 0)

    arrive(0)
    products(steps, up_cols, False, t_buf.at[0], p_buf.at[0], send_sum(0))
    arrive(1)
    products(steps, up_cols, False, t_buf.at[1], p_buf.at[1], send_sum(1))
    lax.fori_loop(0, groups, activate_b, 0)
    arrive(2)
    products(steps, down_rows, True, t_buf.at[2], p_buf.at[2], send_sum(2))
    kept = [
        pltpu.make_async_copy(t_buf.at[1], all_a, out_sem.at[0]),
        pltpu.make_async_copy(t_buf.at[2], all_u, out_sem.at[1]),
    ]
    kept[0].start()
    kept[1].start()
    lax.fori_loop(0, groups, activate_a, 0)
    lax.fori_loop(0, groups, share_a, 0)
    shared(0)
    products(osteps, down_cols, False, g_buf.at[0], o_buf.at[0], send_sibling(0))
    combine(0, groups - 1)
    shared(2)
    products(osteps, up_rows, True, g_buf.at[2], o_buf.at[1], send_sibling(1))
    combine(1, groups - 1)
    kept.append(pltpu.make_async_copy(g_buf.at[2], all_gp, out_sem.at[2]))
    kept[2].start()
    finish(0, out_b)
    shared(1)
    kept.append(pltpu.make_async_copy(g_buf.at[1], all_ga, out_sem.at[3]))
    kept[3].start()
    finish(1, in_grad)

    for c in kept:
        c.wait()
    for s in range(3):
        for c in gather[s][0]:
            c.wait_send()
        gather[s][1].wait_send()
    for c in forwards:
        c.wait_send()
    for s in range(3):
        for k in range(1, nr):
            view = p_buf.at[s, rows_of(rpeer(k), rb), :]
            remote(view, view, rs_send.at[s, k], rg_recv.at[s, k], (rpeer(k), col)).wait_send()
            view = g_buf.at[s, own_rows, :]
            remote(view, view, rg_send.at[s, k], rg_recv.at[s, k], (rpeer(k), col)).wait_send()
    for o in range(2):
        view = sib_buf.at[o]
        remote(view, view, sb_send.at[o], sb_recv.at[o, 0], sibling).wait_send()
        for k in range(1, nz):
            view = o_buf.at[o, rows_of(zpeer(k) * 2 + core, tb), :]
            remote(view, view, zs_send.at[o, k], zs_recv.at[o, 0, k], (row, zpeer(k) * 2 + core)).wait_send()


def exchange(nr, nc, tokens_b, tokens_a, upstream_a, up_weight, down_weight):
    tb, width = tokens_b.shape
    ff = up_weight.shape[1]
    tokens = tb * nc
    rb = tokens // nr
    nz = nc // 2
    chunk = 256
    groups = next(g for g in (6, 4, 3, 2, 1) if (ff // chunk) % g == 0 and (width // chunk) % g == 0)
    dma = pltpu.SemaphoreType.DMA
    anywhere = pl.BlockSpec(memory_space=pl.ANY)
    near = pl.BlockSpec(memory_space=pltpu.VMEM)
    whole = jax.ShapeDtypeStruct((tokens, width), BF)
    hidden = jax.ShapeDtypeStruct((tokens, ff), BF)
    block = jax.ShapeDtypeStruct((tb, width), BF)
    return pl.pallas_call(
        functools.partial(kernel, nr, nc, chunk, groups),
        out_shape=(block, block, whole, whole, hidden, hidden),
        in_specs=[anywhere] * 5,
        out_specs=(near, near, anywhere, anywhere, anywhere, anywhere),
        scratch_shapes=[
            pltpu.VMEM((3, tokens, width), BF),
            pltpu.VMEM((3, tokens, ff), BF),
            pltpu.VMEM((3, nr - 1, rb, ff), BF),
            pltpu.VMEM((3, tokens, ff), BF),
            pltpu.VMEM((2, tokens, width), BF),
            pltpu.VMEM((2, nz, tb, width), BF),
            pltpu.VMEM((2, nz - 1, tb, width), BF),
            pltpu.VMEM((2, max(width, ff), chunk), BF),
            pltpu.VMEM((2, chunk, max(width, ff)), BF),
            dma((3, nz)), dma((3, nz)), dma((3, nz)), dma((3, nz)),
            dma((3, nr)), dma((3, groups, nr)), dma((3, nr)), dma((3, nr)),
            dma((2,)), dma((2, groups)), dma((2, nz)), dma((2, groups, nz)),
            dma((3,)), dma((2,)), dma((4,)),
        ],
        compiler_params=pltpu.CompilerParams(
            collective_id=0, has_side_effects=True, vmem_limit_bytes=62 * 1024 * 1024
        ),
        cost_estimate=pl.CostEstimate(
            flops=10 * tokens * width * ff, bytes_accessed=8 * width * ff, transcendentals=0
        ),
    )(tokens_b, tokens_a, upstream_a, up_weight, down_weight)


def on_device(nr, nc, tokens_b, tokens_a, upstream_a, up_weight, down_weight):
    output_b, input_grad, inputs_a, upstream, gated_a, grad_pre = exchange(
        nr, nc, tokens_b, tokens_a, upstream_a, up_weight, down_weight
    )
    up_grad = lax.dot_general(inputs_a, grad_pre, (((0,), (0,)), ((), ())), preferred_element_type=F32)
    down_grad = lax.dot_general(gated_a, upstream, (((0,), (0,)), ((), ())), preferred_element_type=F32)
    return output_b, input_grad, up_grad.astype(BF), down_grad.astype(BF)


def solution(mesh):
    placed = (P("col", "row"), P("col", "row"), P("col", "row"), P("row", "col"), P("col", "row"))
    return jax.shard_map(
        functools.partial(on_device, mesh.shape["row"], mesh.shape["col"]),
        mesh=mesh,
        in_specs=placed,
        out_specs=(P("col", "row"), P("col", "row"), P("row", "col"), P("col", "row")),
        check_vma=False,
    )
```
